32 devices in a mesh: dp: 8 (over y, x, core), ctx: 4 (over z).
Axes of the slice: x: 2, y: 2, z: 4, core: 2. Of those that a mesh axis runs over, the one named last changes fastest.
Arguments:
- queries: bfloat16 [8, 4, 128, 2048], P('dp', 'ctx'), may hold values from -2.5 to 2.5
- rotated_key_rows: bfloat16 [8, 4, 128, 512], P('dp', 'ctx'), may hold values from -2.5 to 2.5
- values: bfloat16 [8, 4, 128, 512], P('dp', 'ctx'), may hold values from -6 to 6
- cotangent: bfloat16 [8, 4, 128, 2048], P('dp', 'ctx'), may hold values from -6 to 6
- hidden: bfloat16 [8, 4, 128, 4096], P('dp', 'ctx'), may hold values from -6 to 6
- adapter_down_weight: bfloat16 [4096, 16], replicated, may hold values from -0.09375 to 0.09375
- adapter_up_weight: bfloat16 [16, 512], replicated, may hold values from -1.5 to 1.5
- segment_text_length: int32 [8, 4], P('dp', 'ctx'), may hold values from 19 to 78, as said below
Outputs:
- grad_queries: bfloat16 [8, 4, 128, 2048], P('dp', 'ctx')
- grad_keys: bfloat16 [8, 4, 128, 512], P('dp', 'ctx')
- grad_values: bfloat16 [8, 4, 128, 512], P('dp', 'ctx')
- grad_down: float32 [4096, 16], replicated
- grad_up: float32 [16, 512], replicated
The draws below stay inside these ranges and needn't reach their ends.
Inputs may be any that keep to these rules, and one draw needn't show every extreme that they name: `segment_text_length`: every log has a segment with exactly 78 text tokens and another with the fewest.
All inputs are finite; a program needn't handle non-finite values.
Results may differ from the reference program's by a relative error of at most 0.0019.
The reference program's roundings to bfloat16 on the way count: a program that leaves them out, or rounds other values in their place, can miss the bound.
Values may be sent and summed in bfloat16 or wider, within the bound.
A program may use at most 64 MiB of HBM per device.

```python
import math
import jax
import jax.numpy as jnp
from jax import lax

MODEL_WIDTH = 4096
HQ = 16
KEY_VALUE_HEADS = 4
HEAD_SIZE = 128
SUMM = 50
ADAPTER_RANK = 16
TOK_DEV = 128
LOG_COUNT = 8
SEGMENT_COUNT = 4


def draw_segment_text_length(key, part):
    first, second = jax.random.split(key)
    lowest = (TOK_DEV - SUMM) // 4
    highest = TOK_DEV - SUMM
    base = jax.random.randint(first, (LOG_COUNT, SEGMENT_COUNT), lowest, highest + 1)
    chosen = jax.random.randint(second, (LOG_COUNT, 1), 0, SEGMENT_COUNT)
    columns = jnp.arange(SEGMENT_COUNT)[None, :]
    base = jnp.where(columns == chosen, highest, base)
    base = jnp.where(columns == (chosen + 1) % SEGMENT_COUNT, lowest, base)
    return base.astype(jnp.int32)


def steps_of(rng, extent, cuts, low, largest):
    gain, own = 1.0, jax.random.fold_in(rng, 6)
    for dim, shards_of in cuts:
        steps = jnp.exp(jax.random.uniform(jax.random.fold_in(own, dim), (shards_of,), jnp.float32, low / len(cuts), largest / len(cuts)))
        gain = gain * jnp.repeat(steps, extent[dim] // shards_of).reshape([-1 if axis == dim else 1 for axis in range(len(extent))])
    return gain


def bell_draw(stream_key, extent, spread, most, cuts=(), kind=jnp.bfloat16):
    entries = jax.random.normal(stream_key, extent, jnp.float32) * spread
    if len(cuts) > 0:
        entries = steps_of(stream_key, extent, cuts, -0.22, 0.18) * entries
    return jnp.clip(entries, min=-most, max=most).astype(kind)


def setup_inputs(seed: int = 0) -> dict:
    arg_keys = jax.random.split(jax.random.key(seed), 9)
    queries = bell_draw(arg_keys[0], (LOG_COUNT, SEGMENT_COUNT, TOK_DEV, HQ * HEAD_SIZE), 1.0, 2.5, ((0, 8), (1, 4)))
    rotated_key_rows = bell_draw(arg_keys[1], (LOG_COUNT, SEGMENT_COUNT, TOK_DEV, KEY_VALUE_HEADS * HEAD_SIZE), 1.0, 2.5, ((0, 8), (1, 4)))
    values = bell_draw(arg_keys[2], (LOG_COUNT, SEGMENT_COUNT, TOK_DEV, KEY_VALUE_HEADS * HEAD_SIZE), 1.0, 6.0, ((0, 8), (1, 4)))
    cotangent = bell_draw(arg_keys[3], (LOG_COUNT, SEGMENT_COUNT, TOK_DEV, HQ * HEAD_SIZE), 1.0, 6.0, ((0, 8), (1, 4)))
    hidden = bell_draw(arg_keys[4], (LOG_COUNT, SEGMENT_COUNT, TOK_DEV, MODEL_WIDTH), 1.0, 6.0, ((0, 8), (1, 4)))
    adapter_down_weight = bell_draw(arg_keys[5], (MODEL_WIDTH, ADAPTER_RANK), MODEL_WIDTH ** -0.5, 0.09375)
    adapter_up_weight = bell_draw(arg_keys[6], (ADAPTER_RANK, KEY_VALUE_HEADS * HEAD_SIZE), ADAPTER_RANK ** -0.5, 1.5)
    segment_text_length = draw_segment_text_length(jax.random.fold_in(arg_keys[8], 71), 0)
    return dict(queries=queries, rotated_key_rows=rotated_key_rows, values=values, cotangent=cotangent, hidden=hidden, adapter_down_weight=adapter_down_weight, adapter_up_weight=adapter_up_weight, segment_text_length=segment_text_length)


adapter_scale = 2.0

def low_copy(array):
    return lax.optimization_barrier(array.astype(jnp.bfloat16)).astype(jnp.float32)

def segment_grads(query_rows, key_local, value_local, cot_rows, memory_keys, memory_values, memory_owner, position, length):
    tokens = query_rows.shape[0]
    groups = HQ // KEY_VALUE_HEADS
    live = length + SUMM
    rows = jnp.arange(tokens).astype(jnp.int32)
    cot_rows = jnp.where((rows < live)[:, None], cot_rows, jnp.zeros_like(cot_rows))
    local_mask = (rows[None, :] <= rows[:, None]) & (rows[None, :] < live)
    memory_mask = jnp.broadcast_to((memory_owner < position)[None, :], (tokens, memory_owner.shape[0]))
    key_mask = jnp.concatenate([memory_mask, local_mask], axis=1)
    all_keys = jnp.concatenate([memory_keys, key_local], 0).reshape(-1, KEY_VALUE_HEADS, HEAD_SIZE).astype(jnp.float32)
    all_values = jnp.concatenate([memory_values, value_local], 0).reshape(-1, KEY_VALUE_HEADS, HEAD_SIZE).astype(jnp.float32)
    queries = query_rows.reshape(tokens, KEY_VALUE_HEADS, groups, HEAD_SIZE).astype(jnp.float32)
    cotangents = cot_rows.reshape(tokens, KEY_VALUE_HEADS, groups, HEAD_SIZE).astype(jnp.float32)
    softmax_scale = 1.0 / math.sqrt(HEAD_SIZE)
    scores = jnp.einsum('tkgd,mkd->kgtm', queries, all_keys) * softmax_scale
    unnorm = jnp.where(key_mask, jnp.exp(scores), 0.0)
    attend = unnorm / lax.optimization_barrier(jnp.sum(unnorm, -1, keepdims=True))
    attend_grad = jnp.einsum('tkgd,mkd->kgtm', cotangents, all_values)
    row_dot = lax.optimization_barrier(jnp.sum(attend * attend_grad, -1, keepdims=True))
    dscore = low_copy(attend * (attend_grad - row_dot))
    attend_low = low_copy(attend)
    query_grad = jnp.einsum('kgtm,mkd->tkgd', dscore, all_keys) * softmax_scale
    key_grad = jnp.einsum('kgtm,tkgd->mkd', dscore, queries) * softmax_scale
    value_grad = jnp.einsum('kgtm,tkgd->mkd', attend_low, cotangents)
    count = memory_keys.shape[0]
    key_grad = key_grad.reshape(-1, KEY_VALUE_HEADS * HEAD_SIZE)
    value_grad = value_grad.reshape(-1, KEY_VALUE_HEADS * HEAD_SIZE)
    return (query_grad.reshape(tokens, HQ * HEAD_SIZE).astype(jnp.bfloat16), key_grad[:count], key_grad[count:], value_grad[:count], value_grad[count:])

def reference(queries, rotated_key_rows, values, cotangent, hidden, adapter_down_weight, adapter_up_weight, segment_text_length):
    width = KEY_VALUE_HEADS * HEAD_SIZE

    def one_log(inputs):
        query_log, key_log, value_log, cot_log, hidden_log, length_log = inputs

        def take(rows, length):
            return lax.dynamic_slice_in_dim(rows, length, SUMM, 0)
        memory_keys = jax.vmap(take)(key_log, length_log).reshape(SEGMENT_COUNT * SUMM, width)
        memory_values = jax.vmap(take)(value_log, length_log).reshape(SEGMENT_COUNT * SUMM, width)
        memory_owner = (jnp.arange(SEGMENT_COUNT * SUMM) // SUMM).astype(jnp.int32)

        def one_segment(position):
            return segment_grads(query_log[position], key_log[position], value_log[position], cot_log[position], memory_keys, memory_values, memory_owner, position, length_log[position])
        query_grad, memory_key, local_key, memory_value, local_value = lax.map(one_segment, jnp.arange(SEGMENT_COUNT).astype(jnp.int32))
        back_key = lax.optimization_barrier(jnp.sum(memory_key, 0)).reshape(SEGMENT_COUNT, SUMM, width)
        back_value = lax.optimization_barrier(jnp.sum(memory_value, 0)).reshape(SEGMENT_COUNT, SUMM, width)

        def place(local, backward_step, length):
            return local + lax.dynamic_update_slice_in_dim(jnp.zeros_like(local), backward_step, length, 0)
        key_out = jax.vmap(place)(local_key, back_key, length_log).astype(jnp.bfloat16)
        value_result = jax.vmap(place)(local_value, back_value, length_log).astype(jnp.bfloat16)
        hidden_broad = hidden_log.astype(jnp.float32)
        low_rank_state = jnp.einsum('uwx,xe->uwe', hidden_broad, adapter_down_weight.astype(jnp.float32)).astype(jnp.bfloat16)
        backward_step = jnp.einsum('hig,og->hio', value_result.astype(jnp.float32), adapter_up_weight.astype(jnp.float32)).astype(jnp.bfloat16)
        down_part = jnp.einsum('std,str->dr', hidden_broad, backward_step.astype(jnp.float32))
        up_part = jnp.einsum('str,stc->rc', low_rank_state.astype(jnp.float32), value_result.astype(jnp.float32))
        return (query_grad, key_out, value_result, down_part, up_part)
    results = lax.map(one_log, (queries, rotated_key_rows, values, cotangent, hidden, segment_text_length))
    adapter_factor = adapter_scale / (LOG_COUNT * SEGMENT_COUNT)
    return (results[0], results[1], results[2], lax.optimization_barrier(jnp.sum(results[3], 0)) * adapter_factor, lax.optimization_barrier(jnp.sum(results[4], 0)) * adapter_factor)
```

```python
import functools
import math

import jax
import jax.numpy as jnp
from jax import lax
from jax.experimental import pallas as pl
from jax.experimental.pallas import tpu as pltpu
from jax.sharding import PartitionSpec as P

HEAD_SIZE = 128
SUMM = 50
SLOT = 64
BACK = 104
ADAPTER_SCALE = 2.0
MESH = pl.DeviceIdType.MESH
F32 = jnp.float32
BF16 = jnp.bfloat16


def iota(shape, dim):
    return lax.broadcasted_iota(jnp.int32, shape, dim)


def dot(a, b, ca=1, cb=0):
    return lax.dot_general(a, b, (((ca,), (cb,)), ((), ())), preferred_element_type=F32)


def kernel(
    ndp, nctx, kv, groups, tokens, ups_each,
    len_ref, k_hbm, v_hbm, wt_hbm, up_hbm, q_hbm, cot_hbm, hid_hbm,
    gq_hbm, gk_hbm, gv_hbm, down_hbm, upg_hbm,
    gq_ref, gk_ref, gv_ref, down_ref, upg_ref,
    k_ref, v_ref, wt_ref, up_ref, q_ref, cot_ref, hid_ref, hx, bx, own, mem, loc, rcv, mask_ref, s_ref, dp_ref, p_ref, ds_ref,
    pay, rs, zbuf, gat,
    load_sem, store_sem, fs_sem, fr_sem, bs_sem, br_sem, s0, r0, sb, rb, s1, r1, s2, r2, s3, r3,
):
    D = HEAD_SIZE
    nmem = nctx * SLOT
    scale = 1.0 / math.sqrt(D)
    dp = lax.axis_index("dp")
    me = lax.axis_index("ctx")
    loads = [
        pltpu.make_async_copy(src, dst, load_sem.at[i])
        for i, (src, dst) in enumerate((
            (k_hbm, k_ref), (v_hbm, v_ref), (hid_hbm, hid_ref), (wt_hbm, wt_ref),
            (q_hbm, q_ref), (cot_hbm, cot_ref), (up_hbm, up_ref)))
    ]
    for c in loads:
        c.start()
    stores = [
        pltpu.make_async_copy(src, dst, store_sem.at[i])
        for i, (src, dst) in enumerate((
            (gq_ref, gq_hbm), (gk_ref, gk_hbm), (gv_ref, gv_hbm), (down_ref, down_hbm), (upg_ref, upg_hbm)))
    ]

    mem[...] = jnp.zeros_like(mem)
    rcv[...] = jnp.zeros_like(rcv)

    barrier = pltpu.get_barrier_semaphore()
    for k in range(1, ndp):
        pl.semaphore_signal(barrier, inc=1, device_id=(lax.rem(dp + k, ndp), me), device_id_type=MESH)
    for k in range(1, nctx):
        pl.semaphore_signal(barrier, inc=1, device_id=(dp, lax.rem(me + k, nctx)), device_id_type=MESH)

    loads[0].wait()
    loads[1].wait()
    length = len_ref[0, 0]
    live = length + SUMM
    r = iota((SLOT, tokens), 0)
    pick = jnp.where((iota((SLOT, tokens), 1) == length + r) & (r < SUMM), 1.0, 0.0).astype(BF16)
    own_k = dot(pick, k_ref[...]).astype(BF16)
    own_v = dot(pick, v_ref[...]).astype(BF16)
    for h in range(kv):
        own[h, 0:SLOT, :] = own_k[:, h * D:(h + 1) * D]
        own[h, SLOT:2 * SLOT, :] = own_v[:, h * D:(h + 1) * D]

    i = iota((nmem, tokens), 0)
    mask_ref[0:nmem, :] = jnp.where(((i >> 6) < me) & ((i & 63) < SUMM), 1.0, 0.0)
    p = iota((tokens, tokens), 0)
    t = iota((tokens, tokens), 1)
    mask_ref[nmem:nmem + tokens, :] = jnp.where((p <= t) & (p < live), 1.0, 0.0)

    pl.semaphore_wait(barrier, ndp - 1 + nctx - 1)

    def forward(h, k):
        return pltpu.make_async_remote_copy(
            src_ref=own.at[h], dst_ref=mem.at[h, me],
            send_sem=fs_sem.at[h, k], recv_sem=fr_sem.at[h, k],
            device_id=(dp, lax.rem(me + k, nctx)), device_id_type=MESH)

    for h in range(kv):
        for k in range(1, nctx):
            @pl.when(me + k < nctx)
            def _():
                forward(h, k).start()

    chunk = hid_ref.shape[1] // ndp
    loads[2].wait()

    def columns(d):
        return pl.ds(pl.multiple_of(d * chunk, 128), chunk)

    def exchange(k):
        to = lax.rem(dp + k, ndp)
        return pltpu.make_async_remote_copy(
            src_ref=hid_ref.at[:, columns(to)], dst_ref=hx.at[k], send_sem=s0.at[k], recv_sem=r0.at[k],
            device_id=(to, me), device_id_type=MESH)

    for k in range(1, ndp):
        exchange(k).start()

    loads[3].wait()
    low = dot(hid_ref[...], wt_ref[...], 1, 1).astype(BF16)
    loads[4].wait()
    loads[5].wait()
    loads[6].wait()
    row = iota((tokens, D), 0)
    cot_mask = jnp.where(row < live, 1.0, 0.0).astype(BF16)

    def backward(h, j):
        return pltpu.make_async_remote_copy(
            src_ref=loc.at[h, j, pl.ds(0, BACK)], dst_ref=rcv.at[h, j, pl.ds(0, BACK)],
            send_sem=bs_sem.at[h, j], recv_sem=br_sem.at[h, j],
            device_id=(dp, lax.max(me - 1, 0)), device_id_type=MESH)

    def chain(h):
        for j in range(nctx - 1):
            @pl.when((me < nctx - 1) & (j <= me))
            def _():
                backward(h, j).wait_recv()

            @pl.when((me < nctx - 1) & (j < me))
            def _():
                loc[h, j, 0:BACK, :] = loc[h, j, 0:BACK, :] + rcv[h, j, 0:BACK, :]
                backward(h, j).start()

    pr = iota((tokens, 128), 0) - length
    cr = iota((tokens, 128), 1)
    put_k = jnp.where((pr == cr) & (cr < SUMM), 1.0, 0.0).astype(BF16)
    put_v = jnp.where((pr == cr - SUMM) & (pr >= 0) & (pr < SUMM), 1.0, 0.0).astype(BF16)
    key_parts, value_parts = [], []

    def finish(h, back_sum):
        cols = slice(h * D, (h + 1) * D)
        back = rcv[h, me, :, :]
        hi = back.astype(BF16)
        rest = back - hi.astype(F32)
        mid = rest.astype(BF16)
        lo = (rest - mid.astype(F32)).astype(BF16)
        gv = (value_parts[h] + ((dot(put_v, lo) + dot(put_v, mid)) + dot(put_v, hi))).astype(BF16)
        gv_ref[:, cols] = gv
        back_sum = back_sum + dot(up_ref[:, cols], gv, 1, 1)
        gk = key_parts[h] + ((dot(put_k, lo) + dot(put_k, mid)) + dot(put_k, hi))
        gk_ref[:, cols] = gk.astype(BF16)
        up_part = dot(low, gv, 0, 0)
        for a in range(rank // 8):
            n = a * kv + h
            at = (n % ups_each) * 8
            pay[n // ups_each, at:at + 8, :] = up_part[a * 8:a * 8 + 8]
        return back_sum

    rank = up_ref.shape[0]
    back_sum = jnp.zeros((rank, tokens), F32)
    for n in range(rank // 8 * kv, ndp * ups_each):
        at = (n % ups_each) * 8
        pay[n // ups_each, at:at + 8, :] = jnp.zeros((8, 128), F32)

    for h in range(kv):
        for k in range(1, nctx):
            @pl.when(me >= k)
            def _():
                forward(h, k).wait_recv()
        cols = slice(h * D, (h + 1) * D)
        keys = jnp.concatenate([mem[h, j, 0:SLOT, :] for j in range(nctx)] + [k_ref[:, cols]], 0)
        vals = jnp.concatenate([mem[h, j, SLOT:2 * SLOT, :] for j in range(nctx)] + [v_ref[:, cols]], 0)
        heads = [h * groups + g for g in range(groups)]
        q = jnp.concatenate([q_ref[:, a * D:(a + 1) * D] for a in heads], 0)
        c = jnp.concatenate([cot_ref[:, a * D:(a + 1) * D] * cot_mask for a in heads], 0)
        s_ref[...] = dot(keys, q, 1, 1)
        dp_ref[...] = dot(vals, c, 1, 1)
        for g in range(groups):
            lanes = slice(g * tokens, (g + 1) * tokens)
            e = jnp.exp(s_ref[:, lanes] * scale) * mask_ref[...]
            attend = e * (1.0 / jnp.sum(e, 0, keepdims=True))
            grad = dp_ref[:, lanes]
            dot_row = jnp.sum(attend * grad, 0, keepdims=True)
            p_ref[:, lanes] = attend.astype(BF16)
            ds_ref[:, lanes] = (attend * (grad - dot_row)).astype(BF16)
        ds = ds_ref[...]
        dk = dot(ds, q) * scale
        dv = dot(p_ref[...], c)
        for j in range(nctx - 1):
            at = j * SLOT
            tail = pltpu.roll(dv[at:at + SLOT], 2, 0)
            loc[h, j, 0:48, :] = dk[at:at + 48]
            loc[h, j, 48:56, :] = dk[at + 48:at + 56] + tail[0:8]
            loc[h, j, 56:BACK, :] = tail[8:56]

            @pl.when(me == nctx - 1)
            def _():
                backward(h, j).start()
        key_parts.append(dk[nmem:])
        value_parts.append(dv[nmem:])
        dq = dot(ds, keys, 0, 0) * scale
        for g, a in enumerate(heads):
            gq_ref[:, a * D:(a + 1) * D] = dq[g * tokens:(g + 1) * tokens].astype(BF16)
        if h > 0:
            chain(h - 1)
            back_sum = finish(h - 1, back_sum)
    stores[0].start()
    chain(kv - 1)
    back_sum = finish(kv - 1, back_sum)

    bx[0] = back_sum.astype(BF16)

    def tell(k):
        return pltpu.make_async_remote_copy(
            src_ref=bx.at[0], dst_ref=bx.at[k], send_sem=sb.at[k], recv_sem=rb.at[k],
            device_id=(lax.rem(dp + k, ndp), me), device_id_type=MESH)

    def scatter(k):
        to = lax.rem(dp + k, ndp)
        return pltpu.make_async_remote_copy(
            src_ref=pay.at[to], dst_ref=rs.at[k], send_sem=s1.at[k], recv_sem=r1.at[k],
            device_id=(to, me), device_id_type=MESH)

    def spread(k):
        return pltpu.make_async_remote_copy(
            src_ref=zbuf.at[me], dst_ref=zbuf.at[me], send_sem=s2.at[k], recv_sem=r2.at[k],
            device_id=(dp, lax.rem(me + k, nctx)), device_id_type=MESH)

    def spread_in(k):
        come = lax.rem(me + nctx - k, nctx)
        return pltpu.make_async_remote_copy(
            src_ref=zbuf.at[come], dst_ref=zbuf.at[come], send_sem=s2.at[k], recv_sem=r2.at[k],
            device_id=(dp, come), device_id_type=MESH)

    def gather(k):
        return pltpu.make_async_remote_copy(
            src_ref=gat.at[dp], dst_ref=gat.at[dp], send_sem=s3.at[k], recv_sem=r3.at[k],
            device_id=(lax.rem(dp + k, ndp), me), device_id_type=MESH)

    def gather_in(k):
        come = lax.rem(dp + ndp - k, ndp)
        return pltpu.make_async_remote_copy(
            src_ref=gat.at[come], dst_ref=gat.at[come], send_sem=s3.at[k], recv_sem=r3.at[k],
            device_id=(come, me), device_id_type=MESH)

    for k in range(1, ndp):
        tell(k).start()
    for k in range(1, ndp):
        scatter(k).start()
    stores[1].start()
    stores[2].start()
    down = dot(bx[0], hid_ref[:, columns(dp)])
    up_sum = pay[dp]
    for k in range(1, ndp):
        exchange(k).wait_recv()
        tell(k).wait_recv()
        down = down + dot(bx[k], hx[k])
    for k in range(1, ndp):
        scatter(k).wait_recv()
        up_sum = up_sum + rs[k]
    blocks = chunk // 128
    for b in range(blocks):
        zbuf[me, b * rank:(b + 1) * rank, :] = down[:, b * 128:(b + 1) * 128]
    zbuf[me, blocks * rank:blocks * rank + ups_each * 8, :] = up_sum
    for k in range(1, nctx):
        spread(k).start()
    for k in range(1, nctx):
        spread_in(k).wait_recv()
    total = zbuf[0]
    for j in range(1, nctx):
        total = total + zbuf[j]
    gat[dp] = total * (ADAPTER_SCALE / (ndp * nctx))
    for k in range(1, ndp):
        gather(k).start()
    for d in range(ndp):
        if d < ndp - 1:
            gather_in(d + 1).wait_recv()
    for d in range(ndp):
        for b in range(blocks):
            at = d * chunk + b * 128
            down_ref[:, at:at + 128] = gat[d, b * rank:(b + 1) * rank, :]
        for u in range(ups_each):
            n = d * ups_each + u
            if n < rank // 8 * kv:
                at = blocks * rank + u * 8
                a, b = n // kv * 8, n % kv * 128
                upg_ref[a:a + 8, b:b + 128] = gat[d, at:at + 8, :]

    stores[3].start()
    stores[4].start()

    for h in range(kv):
        for k in range(1, nctx):
            @pl.when(me + k < nctx)
            def _():
                forward(h, k).wait_send()
        for j in range(nctx - 1):
            @pl.when(j < me)
            def _():
                backward(h, j).wait_send()
    for k in range(1, ndp):
        exchange(k).wait_send()
        tell(k).wait_send()
        scatter(k).wait_send()
        gather(k).wait_send()
    for k in range(1, nctx):
        spread(k).wait_send()
    for c in stores:
        c.wait()


def write_out(*refs):
    sems = refs[10]
    copies = [pltpu.make_async_copy(refs[i], refs[i + 5], sems.at[i]) for i in range(5)]
    for c in copies:
        c.start()
    for c in copies:
        c.wait()


def per_device(ndp, nctx, queries, rotated_key_rows, values, cotangent, hidden, down_w, up_w, seg_len):
    q, k, v, cot, hid = (a[0, 0] for a in (queries, rotated_key_rows, values, cotangent, hidden))
    tokens, width = k.shape
    kv = width // HEAD_SIZE
    groups = q.shape[1] // width
    model = hid.shape[1]
    rank = up_w.shape[0]
    D = HEAD_SIZE
    ups_each = -(-(rank // 8 * kv) // ndp)
    chunk = model // ndp
    rows = chunk // 128 * rank + ups_each * 8
    nkeys = nctx * SLOT + tokens
    lanes = groups * tokens
    hbm = pl.BlockSpec(memory_space=pl.ANY)
    sm = pl.BlockSpec(memory_space=pltpu.SMEM)
    dma = pltpu.SemaphoreType.DMA
    results = pl.pallas_call(
        functools.partial(kernel, ndp, nctx, kv, groups, tokens, ups_each),
        out_shape=(
            jax.ShapeDtypeStruct(q.shape, BF16),
            jax.ShapeDtypeStruct(k.shape, BF16),
            jax.ShapeDtypeStruct(v.shape, BF16),
            jax.ShapeDtypeStruct((rank, model), F32),
            jax.ShapeDtypeStruct((rank, width), F32),
        ),
        in_specs=[sm] + [hbm] * 7,
        out_specs=(hbm,) * 5,
        scratch_shapes=[
            pltpu.VMEM(q.shape, BF16),
            pltpu.VMEM(k.shape, BF16),
            pltpu.VMEM(v.shape, BF16),
            pltpu.VMEM((rank, model), F32),
            pltpu.VMEM((rank, width), F32),
            pltpu.VMEM(k.shape, BF16),
            pltpu.VMEM(v.shape, BF16),
            pltpu.VMEM((rank, model), BF16),
            pltpu.VMEM((rank, width), BF16),
            pltpu.VMEM(q.shape, BF16),
            pltpu.VMEM(cot.shape, BF16),
            pltpu.VMEM(hid.shape, BF16),
            pltpu.VMEM((ndp, tokens, chunk), BF16),
            pltpu.VMEM((ndp, rank, tokens), BF16),
            pltpu.VMEM((kv, 2 * SLOT, D), BF16),
            pltpu.VMEM((kv, nctx, 2 * SLOT, D), BF16),
            pltpu.VMEM((kv, nctx, 128, D), F32),
            pltpu.VMEM((kv, nctx, 128, D), F32),
            pltpu.VMEM((nkeys, tokens), F32),
            pltpu.VMEM((nkeys, lanes), F32),
            pltpu.VMEM((nkeys, lanes), F32),
            pltpu.VMEM((nkeys, lanes), BF16),
            pltpu.VMEM((nkeys, lanes), BF16),
            pltpu.VMEM((ndp, ups_each * 8, 128), F32),
            pltpu.VMEM((ndp, ups_each * 8, 128), F32),
            pltpu.VMEM((nctx, rows, 128), F32),
            pltpu.VMEM((ndp, rows, 128), F32),
            dma((7,)), dma((5,)),
            dma((kv, nctx)), dma((kv, nctx)),
            dma((kv, nctx)), dma((kv, nctx)),
            dma((ndp,)), dma((ndp,)),
            dma((ndp,)), dma((ndp,)),
            dma((ndp,)), dma((ndp,)),
            dma((nctx,)), dma((nctx,)),
            dma((ndp,)), dma((ndp,)),
        ],
        compiler_params=pltpu.CompilerParams(
            collective_id=0, has_side_effects=True, vmem_limit_bytes=62 * 1024 * 1024),
    )(seg_len, k, v, down_w.T, up_w, q, cot, hid)
    gq, gk, gv, down, upg = pl.pallas_call(
        write_out,
        out_shape=tuple(jax.ShapeDtypeStruct(a.shape, a.dtype) for a in results),
        in_specs=[hbm] * 5,
        out_specs=(hbm,) * 5,
        scratch_shapes=[dma((5,))],
        compiler_params=pltpu.CompilerParams(vmem_limit_bytes=62 * 1024 * 1024),
    )(*results)
    return gq[None, None], gk[None, None], gv[None, None], down.T, upg


def solution(mesh):
    split = P("dp", "ctx", None, None)
    return jax.shard_map(
        functools.partial(per_device, mesh.shape["dp"], mesh.shape["ctx"]),
        mesh=mesh,
        in_specs=(split,) * 5 + (P(), P(), P("dp", "ctx")),
        out_specs=(split,) * 3 + (P(), P()),
        check_vma=False,
    )
```

```python
import functools
import math

import jax
import jax.numpy as jnp
from jax import lax
from jax.experimental import pallas as pl
from jax.experimental.pallas import tpu as pltpu
from jax.sharding import PartitionSpec as P

HEAD_SIZE = 128
SUMM = 50
SLOT = 64
BACK = 104
ADAPTER_SCALE = 2.0
MESH = pl.DeviceIdType.MESH
F32 = jnp.float32
BF16 = jnp.bfloat16


def iota(shape, dim):
    return lax.broadcasted_iota(jnp.int32, shape, dim)


def dot(a, b, ca=1, cb=0):
    return lax.dot_general(a, b, (((ca,), (cb,)), ((), ())), preferred_element_type=F32)


def kernel(
    ndp, nctx, kv, groups, tokens, ups_each,
    len_ref, k_hbm, v_hbm, wt_hbm, up_hbm, q_hbm, cot_hbm, hid_hbm,
    gq_hbm, gk_hbm, gv_hbm, down_hbm, upg_hbm,
    gq_ref, gk_ref, gv_ref, down_ref, upg_ref,
    k_ref, v_ref, wt_ref, up_ref, q_ref, cot_ref, hid_ref, hx, bx, own, mem, loc, rcv, mask_ref, s_ref, dp_ref, p_ref, ds_ref,
    pay, rs, zbuf, gat,
    load_sem, store_sem, fs_sem, fr_sem, bs_sem, br_sem, s0, r0, sb, rb, s1, r1, s2, r2, s3, r3,
):
    D = HEAD_SIZE
    nmem = nctx * SLOT
    scale = 1.0 / math.sqrt(D)
    dp = lax.axis_index("dp")
    me = lax.axis_index("ctx")
    loads = [
        pltpu.make_async_copy(src, dst, load_sem.at[i])
        for i, (src, dst) in enumerate((
            (k_hbm, k_ref), (v_hbm, v_ref), (hid_hbm, hid_ref), (wt_hbm, wt_ref),
            (q_hbm, q_ref), (cot_hbm, cot_ref), (up_hbm, up_ref)))
    ]
    for c in loads:
        c.start()
    stores = [
        pltpu.make_async_copy(src, dst, store_sem.at[i])
        for i, (src, dst) in enumerate((
            (gq_ref, gq_hbm), (gk_ref, gk_hbm), (gv_ref, gv_hbm), (down_ref, down_hbm), (upg_ref, upg_hbm)))
    ]

    mem[...] = jnp.zeros_like(mem)
    rcv[...] = jnp.zeros_like(rcv)

    barrier = pltpu.get_barrier_semaphore()
    for k in range(1, ndp):
        pl.semaphore_signal(barrier, inc=1, device_id=(lax.rem(dp + k, ndp), me), device_id_type=MESH)
    for k in range(1, nctx):
        pl.semaphore_signal(barrier, inc=1, device_id=(dp, lax.rem(me + k, nctx)), device_id_type=MESH)

    loads[0].wait()
    loads[1].wait()
    length = len_ref[0, 0]
    live = length + SUMM
    r = iota((SLOT, tokens), 0)
    pick = jnp.where((iota((SLOT, tokens), 1) == length + r) & (r < SUMM), 1.0, 0.0).astype(BF16)
    own_k = dot(pick, k_ref[...]).astype(BF16)
    own_v = dot(pick, v_ref[...]).astype(BF16)
    for h in range(kv):
        own[h, 0:SLOT, :] = own_k[:, h * D:(h + 1) * D]
        own[h, SLOT:2 * SLOT, :] = own_v[:, h * D:(h + 1) * D]

    i = iota((nmem, tokens), 0)
    mask_ref[0:nmem, :] = jnp.where(((i >> 6) < me) & ((i & 63) < SUMM), 1.0, 0.0)
    p = iota((tokens, tokens), 0)
    t = iota((tokens, tokens), 1)
    mask_ref[nmem:nmem + tokens, :] = jnp.where((p <= t) & (p < live), 1.0, 0.0)

    pl.semaphore_wait(barrier, ndp - 1 + nctx - 1)

    def forward(h, k):
        return pltpu.make_async_remote_copy(
            src_ref=own.at[h], dst_ref=mem.at[h, me],
            send_sem=fs_sem.at[h, k], recv_sem=fr_sem.at[h, k],
            device_id=(dp, lax.rem(me + k, nctx)), device_id_type=MESH)

    for h in range(kv):
        for k in range(1, nctx):
            @pl.when(me + k < nctx)
            def _():
                forward(h, k).start()

    chunk = hid_ref.shape[1] // ndp
    loads[2].wait()

    def columns(d):
        return pl.ds(pl.multiple_of(d * chunk, 128), chunk)

    def exchange(k):
        to = lax.rem(dp + k, ndp)
        return pltpu.make_async_remote_copy(
            src_ref=hid_ref.at[:, columns(to)], dst_ref=hx.at[k], send_sem=s0.at[k], recv_sem=r0.at[k],
            device_id=(to, me), device_id_type=MESH)

    for k in range(1, ndp):
        exchange(k).start()

    loads[3].wait()
    low = dot(hid_ref[...], wt_ref[...], 1, 1).astype(BF16)
    loads[4].wait()
    loads[5].wait()
    loads[6].wait()
    row = iota((tokens, D), 0)
    cot_mask = jnp.where(row < live, 1.0, 0.0).astype(BF16)

    def backward(h, j):
        return pltpu.make_async_remote_copy(
            src_ref=loc.at[h, j, pl.ds(0, BACK)], dst_ref=rcv.at[h, j, pl.ds(0, BACK)],
            send_sem=bs_sem.at[h, j], recv_sem=br_sem.at[h, j],
            device_id=(dp, lax.max(me - 1, 0)), device_id_type=MESH)

    def chain(h):
        for j in range(nctx - 1):
            @pl.when((me < nctx - 1) & (j <= me))
            def _():
                backward(h, j).wait_recv()

            @pl.when((me < nctx - 1) & (j < me))
            def _():
                loc[h, j, 0:BACK, :] = loc[h, j, 0:BACK, :] + rcv[h, j, 0:BACK, :]
                backward(h, j).start()

    pr = iota((tokens, 128), 0) - length
    cr = iota((tokens, 128), 1)
    put_k = jnp.where((pr == cr) & (cr < SUMM), 1.0, 0.0).astype(BF16)
    put_v = jnp.where((pr == cr - SUMM) & (pr >= 0) & (pr < SUMM), 1.0, 0.0).astype(BF16)
    key_parts, value_parts = [], []

    def finish(h, back_sum):
        cols = slice(h * D, (h + 1) * D)
        back = rcv[h, me, :, :]
        hi = back.astype(BF16)
        rest = back - hi.astype(F32)
        mid = rest.astype(BF16)
        lo = (rest - mid.astype(F32)).astype(BF16)
        gv = (value_parts[h] + ((dot(put_v, lo) + dot(put_v, mid)) + dot(put_v, hi))).astype(BF16)
        gv_ref[:, cols] = gv
        back_sum = back_sum + dot(up_ref[:, cols], gv, 1, 1)
        gk = key_parts[h] + ((dot(put_k, lo) + dot(put_k, mid)) + dot(put_k, hi))
        gk_ref[:, cols] = gk.astype(BF16)
        up_part = dot(low, gv, 0, 0)
        for a in range(rank // 8):
            n = a * kv + h
            at = (n % ups_each) * 8
            pay[n // ups_each, at:at + 8, :] = up_part[a * 8:a * 8 + 8]
        return back_sum

    rank = up_ref.shape[0]
    back_sum = jnp.zeros((rank, tokens), F32)
    for n in range(rank // 8 * kv, ndp * ups_each):
        at = (n % ups_each) * 8
        pay[n // ups_each, at:at + 8, :] = jnp.zeros((8, 128), F32)

    for h in range(kv):
        for k in range(1, nctx):
            @pl.when(me >= k)
            def _():
                forward(h, k).wait_recv()
        cols = slice(h * D, (h + 1) * D)
        keys = jnp.concatenate([mem[h, j, 0:SLOT, :] for j in range(nctx)] + [k_ref[:, cols]], 0)
        vals = jnp.concatenate([mem[h, j, SLOT:2 * SLOT, :] for j in range(nctx)] + [v_ref[:, cols]], 0)
        heads = [h * groups + g for g in range(groups)]
        q = jnp.concatenate([q_ref[:, a * D:(a + 1) * D] for a in heads], 0)
        c = jnp.concatenate([cot_ref[:, a * D:(a + 1) * D] * cot_mask for a in heads], 0)
        s_ref[...] = dot(keys, q, 1, 1)
        dp_ref[...] = dot(vals, c, 1, 1)
        for g in range(groups):
            lanes = slice(g * tokens, (g + 1) * tokens)
            e = jnp.exp(s_ref[:, lanes] * scale) * mask_ref[...]
            attend = e * (1.0 / jnp.sum(e, 0, keepdims=True))
            grad = dp_ref[:, lanes]
            dot_row = jnp.sum(attend * grad, 0, keepdims=True)
            p_ref[:, lanes] = attend.astype(BF16)
            ds_ref[:, lanes] = (attend * (grad - dot_row)).astype(BF16)
        ds = ds_ref[...]
        dk = dot(ds, q) * scale
        dv = dot(p_ref[...], c)
        for j in range(nctx - 1):
            at = j * SLOT
            tail = pltpu.roll(dv[at:at + SLOT], 2, 0)
            loc[h, j, 0:48, :] = dk[at:at + 48]
            loc[h, j, 48:56, :] = dk[at + 48:at + 56] + tail[0:8]
            loc[h, j, 56:BACK, :] = tail[8:56]

            @pl.when(me == nctx - 1)
            def _():
                backward(h, j).start()
        key_parts.append(dk[nmem:])
        value_parts.append(dv[nmem:])
        dq = dot(ds, keys, 0, 0) * scale
        for g, a in enumerate(heads):
            gq_ref[:, a * D:(a + 1) * D] = dq[g * tokens:(g + 1) * tokens].astype(BF16)
        if h > 0:
            chain(h - 1)
            back_sum = finish(h - 1, back_sum)
    stores[0].start()
    chain(kv - 1)
    back_sum = finish(kv - 1, back_sum)

    bx[0] = back_sum.astype(BF16)

    def tell(k):
        return pltpu.make_async_remote_copy(
            src_ref=bx.at[0], dst_ref=bx.at[k], send_sem=sb.at[k], recv_sem=rb.at[k],
            device_id=(lax.rem(dp + k, ndp), me), device_id_type=MESH)

    def scatter(k):
        to = lax.rem(dp + k, ndp)
        return pltpu.make_async_remote_copy(
            src_ref=pay.at[to], dst_ref=rs.at[k], send_sem=s1.at[k], recv_sem=r1.at[k],
            device_id=(to, me), device_id_type=MESH)

    def spread(k):
        return pltpu.make_async_remote_copy(
            src_ref=zbuf.at[me], dst_ref=zbuf.at[me], send_sem=s2.at[k], recv_sem=r2.at[k],
            device_id=(dp, lax.rem(me + k, nctx)), device_id_type=MESH)

    def spread_in(k):
        come = lax.rem(me + nctx - k, nctx)
        return pltpu.make_async_remote_copy(
            src_ref=zbuf.at[come], dst_ref=zbuf.at[come], send_sem=s2.at[k], recv_sem=r2.at[k],
            device_id=(dp, come), device_id_type=MESH)

    def gather(k):
        return pltpu.make_async_remote_copy(
            src_ref=gat.at[dp], dst_ref=gat.at[dp], send_sem=s3.at[k], recv_sem=r3.at[k],
            device_id=(lax.rem(dp + k, ndp), me), device_id_type=MESH)

    def gather_in(k):
        come = lax.rem(dp + ndp - k, ndp)
        return pltpu.make_async_remote_copy(
            src_ref=gat.at[come], dst_ref=gat.at[come], send_sem=s3.at[k], recv_sem=r3.at[k],
            device_id=(come, me), device_id_type=MESH)

    for k in range(1, ndp):
        tell(k).start()
    for k in range(1, ndp):
        scatter(k).start()
    stores[1].start()
    stores[2].start()
    down = dot(bx[0], hid_ref[:, columns(dp)])
    up_sum = pay[dp]
    for k in range(1, ndp):
        exchange(k).wait_recv()
        tell(k).wait_recv()
        down = down + dot(bx[k], hx[k])
    for k in range(1, ndp):
        scatter(k).wait_recv()
        up_sum = up_sum + rs[k]
    blocks = chunk // 128
    for b in range(blocks):
        zbuf[me, b * rank:(b + 1) * rank, :] = down[:, b * 128:(b + 1) * 128]
    zbuf[me, blocks * rank:blocks * rank + ups_each * 8, :] = up_sum
    for k in range(1, nctx):
        spread(k).start()
    for k in range(1, nctx):
        spread_in(k).wait_recv()
    total = zbuf[0]
    for j in range(1, nctx):
        total = total + zbuf[j]
    gat[dp] = total * (ADAPTER_SCALE / (ndp * nctx))
    for k in range(1, ndp):
        gather(k).start()
    for d in range(ndp):
        if d < ndp - 1:
            gather_in(d + 1).wait_recv()
    for d in range(ndp):
        for b in range(blocks):
            at = d * chunk + b * 128
            down_ref[:, at:at + 128] = gat[d, b * rank:(b + 1) * rank, :]
        for u in range(ups_each):
            n = d * ups_each + u
            if n < rank // 8 * kv:
                at = blocks * rank + u * 8
                a, b = n // kv * 8, n % kv * 128
                upg_ref[a:a + 8, b:b + 128] = gat[d, at:at + 8, :]

    stores[3].start()
    stores[4].start()

    for h in range(kv):
        for k in range(1, nctx):
            @pl.when(me + k < nctx)
            def _():
                forward(h, k).wait_send()
        for j in range(nctx - 1):
            @pl.when(j < me)
            def _():
                backward(h, j).wait_send()
    for k in range(1, ndp):
        exchange(k).wait_send()
        tell(k).wait_send()
        scatter(k).wait_send()
        gather(k).wait_send()
    for k in range(1, nctx):
        spread(k).wait_send()
    for c in stores:
        c.wait()


def write_out(*refs):
    ins, outs, held, sem_in, sem_out = refs[:5], refs[5:10], refs[10:15], refs[15], refs[16]
    loads = [pltpu.make_async_copy(ins[i], held[i], sem_in.at[i]) for i in range(5)]
    stores = [pltpu.make_async_copy(held[i], outs[i], sem_out.at[i]) for i in range(5)]
    for c in loads:
        c.start()
    for i in range(5):
        loads[i].wait()
        stores[i].start()
    for c in stores:
        c.wait()


def per_device(ndp, nctx, queries, rotated_key_rows, values, cotangent, hidden, down_w, up_w, seg_len):
    q, k, v, cot, hid = (a[0, 0] for a in (queries, rotated_key_rows, values, cotangent, hidden))
    tokens, width = k.shape
    kv = width // HEAD_SIZE
    groups = q.shape[1] // width
    model = hid.shape[1]
    rank = up_w.shape[0]
    D = HEAD_SIZE
    ups_each = -(-(rank // 8 * kv) // ndp)
    chunk = model // ndp
    rows = chunk // 128 * rank + ups_each * 8
    nkeys = nctx * SLOT + tokens
    lanes = groups * tokens
    hbm = pl.BlockSpec(memory_space=pl.ANY)
    sm = pl.BlockSpec(memory_space=pltpu.SMEM)
    dma = pltpu.SemaphoreType.DMA
    results = pl.pallas_call(
        functools.partial(kernel, ndp, nctx, kv, groups, tokens, ups_each),
        out_shape=(
            jax.ShapeDtypeStruct(q.shape, BF16),
            jax.ShapeDtypeStruct(k.shape, BF16),
            jax.ShapeDtypeStruct(v.shape, BF16),
            jax.ShapeDtypeStruct((rank, model), F32),
            jax.ShapeDtypeStruct((rank, width), F32),
        ),
        in_specs=[sm] + [hbm] * 7,
        out_specs=(hbm,) * 5,
        scratch_shapes=[
            pltpu.VMEM(q.shape, BF16),
            pltpu.VMEM(k.shape, BF16),
            pltpu.VMEM(v.shape, BF16),
            pltpu.VMEM((rank, model), F32),
            pltpu.VMEM((rank, width), F32),
            pltpu.VMEM(k.shape, BF16),
            pltpu.VMEM(v.shape, BF16),
            pltpu.VMEM((rank, model), BF16),
            pltpu.VMEM((rank, width), BF16),
            pltpu.VMEM(q.shape, BF16),
            pltpu.VMEM(cot.shape, BF16),
            pltpu.VMEM(hid.shape, BF16),
            pltpu.VMEM((ndp, tokens, chunk), BF16),
            pltpu.VMEM((ndp, rank, tokens), BF16),
            pltpu.VMEM((kv, 2 * SLOT, D), BF16),
            pltpu.VMEM((kv, nctx, 2 * SLOT, D), BF16),
            pltpu.VMEM((kv, nctx, 128, D), F32),
            pltpu.VMEM((kv, nctx, 128, D), F32),
            pltpu.VMEM((nkeys, tokens), F32),
            pltpu.VMEM((nkeys, lanes), F32),
            pltpu.VMEM((nkeys, lanes), F32),
            pltpu.VMEM((nkeys, lanes), BF16),
            pltpu.VMEM((nkeys, lanes), BF16),
            pltpu.VMEM((ndp, ups_each * 8, 128), F32),
            pltpu.VMEM((ndp, ups_each * 8, 128), F32),
            pltpu.VMEM((nctx, rows, 128), F32),
            pltpu.VMEM((ndp, rows, 128), F32),
            dma((7,)), dma((5,)),
            dma((kv, nctx)), dma((kv, nctx)),
            dma((kv, nctx)), dma((kv, nctx)),
            dma((ndp,)), dma((ndp,)),
            dma((ndp,)), dma((ndp,)),
            dma((ndp,)), dma((ndp,)),
            dma((nctx,)), dma((nctx,)),
            dma((ndp,)), dma((ndp,)),
        ],
        compiler_params=pltpu.CompilerParams(
            collective_id=0, has_side_effects=True, vmem_limit_bytes=62 * 1024 * 1024),
    )(seg_len, k, v, down_w.T, up_w, q, cot, hid)
    gq, gk, gv, down, upg = pl.pallas_call(
        write_out,
        out_shape=tuple(jax.ShapeDtypeStruct(a.shape, a.dtype) for a in results),
        in_specs=[hbm] * 5,
        out_specs=(hbm,) * 5,
        scratch_shapes=[pltpu.VMEM(a.shape, a.dtype) for a in results] + [dma((5,)), dma((5,))],
        compiler_params=pltpu.CompilerParams(vmem_limit_bytes=62 * 1024 * 1024),
    )(*results)
    return gq[None, None], gk[None, None], gv[None, None], down.T, upg


def solution(mesh):
    split = P("dp", "ctx", None, None)
    return jax.shard_map(
        functools.partial(per_device, mesh.shape["dp"], mesh.shape["ctx"]),
        mesh=mesh,
        in_specs=(split,) * 5 + (P(), P(), P("dp", "ctx")),
        out_specs=(split,) * 3 + (P(), P()),
        check_vma=False,
    )
```

```python
import functools
import math

import jax
import jax.numpy as jnp
from jax import lax
from jax.experimental import pallas as pl
from jax.experimental.pallas import tpu as pltpu
from jax.sharding import PartitionSpec as P

HEAD_SIZE = 128
SUMM = 50
SLOT = 64
BACK = 112
STEPS = 64.0
TOP = 32000.0
ADAPTER_SCALE = 2.0
MESH = pl.DeviceIdType.MESH
F32 = jnp.float32
BF16 = jnp.bfloat16


def iota(shape, dim):
    return lax.broadcasted_iota(jnp.int32, shape, dim)


def dot(a, b, ca=1, cb=0):
    return lax.dot_general(a, b, (((ca,), (cb,)), ((), ())), preferred_element_type=F32)


def code(x):
    most = jnp.max(jnp.abs(x), 0, keepdims=True)
    level = jnp.ceil(jnp.log(jnp.maximum(most, 1e-30)) * (STEPS / math.log(2.0))) + 1.0
    return jnp.round(x * (TOP * jnp.exp(level * (-math.log(2.0) / STEPS)))), level


def scale_of(level):
    return jnp.exp(level * (math.log(2.0) / STEPS)) * (1.0 / TOP)


def level_rows(first, second, rows):
    at = iota((rows, 128), 0)
    return jnp.where(at == 0, first, jnp.where(at == 1, second, 0.0))


def to_wire(x):
    return x.astype(jnp.int32).astype(jnp.int16)


def from_wire(x):
    return x.astype(jnp.int32).astype(F32)


def pack_terms(both):
    k, level_k = code(both[0:SLOT])
    v, level_v = code(both[SLOT:2 * SLOT])
    v = pltpu.roll(v, 2, 0)
    return to_wire(jnp.concatenate(
        [k[0:48], k[48:56] + v[0:8], v[8:56], level_rows(level_k, level_v, 8)], 0))


def unpack_terms(wire):
    x = from_wire(wire)
    keep = iota((SLOT, 128), 0) < SUMM
    k = jnp.where(keep, x[0:SLOT] * scale_of(x[104:105]), 0.0)
    v = jnp.where(keep, pltpu.roll(x[48:112], SLOT - 2, 0) * scale_of(x[105:106]), 0.0)
    return jnp.concatenate([k, v], 0)


def pack_sums(x, first):
    a, level_a = code(x[:first])
    b, level_b = code(x[first:])
    wire = [a, b, level_rows(level_a, level_b, 8)]
    if (x.shape[0] + 8) % 16:
        wire.append(jnp.zeros((8, 128), F32))
    return to_wire(jnp.concatenate(wire, 0))


def unpack_sums(wire, first, rows):
    x = from_wire(wire)
    return jnp.concatenate(
        [x[:first] * scale_of(x[rows:rows + 1]), x[first:rows] * scale_of(x[rows + 1:rows + 2])], 0)


def kernel(
    ndp, nctx, kv, groups, tokens, ups_each,
    len_ref, k_hbm, v_hbm, wt_hbm, up_hbm, q_hbm, cot_hbm, hid_hbm,
    gq_hbm, gk_hbm, gv_hbm, down_hbm, upg_hbm,
    gq_ref, gk_ref, gv_ref, down_ref, upg_ref,
    k_ref, v_ref, wt_ref, up_ref, q_ref, cot_ref, hid_ref, hx, bx, own, mem, loc, out, rcv, mask_ref, s_ref, dp_ref, p_ref, ds_ref,
    pay, rs, zbuf, gat,
    load_sem, store_sem, fs_sem, fr_sem, bs_sem, br_sem, s0, r0, sb, rb, s1, r1, s2, r2, s3, r3,
):
    D = HEAD_SIZE
    nmem = nctx * SLOT
    scale = 1.0 / math.sqrt(D)
    dp = lax.axis_index("dp")
    me = lax.axis_index("ctx")
    loads = [
        pltpu.make_async_copy(src, dst, load_sem.at[i])
        for i, (src, dst) in enumerate((
            (k_hbm, k_ref), (v_hbm, v_ref), (hid_hbm, hid_ref), (wt_hbm, wt_ref),
            (q_hbm, q_ref), (cot_hbm, cot_ref), (up_hbm, up_ref)))
    ]
    for c in loads:
        c.start()
    stores = [
        pltpu.make_async_copy(src, dst, store_sem.at[i])
        for i, (src, dst) in enumerate((
            (gq_ref, gq_hbm), (gk_ref, gk_hbm), (gv_ref, gv_hbm), (down_ref, down_hbm), (upg_ref, upg_hbm)))
    ]

    mem[...] = jnp.zeros_like(mem)
    rcv[...] = jnp.zeros_like(rcv)

    barrier = pltpu.get_barrier_semaphore()
    for k in range(1, ndp):
        pl.semaphore_signal(barrier, inc=1, device_id=(lax.rem(dp + k, ndp), me), device_id_type=MESH)
    for k in range(1, nctx):
        pl.semaphore_signal(barrier, inc=1, device_id=(dp, lax.rem(me + k, nctx)), device_id_type=MESH)

    loads[0].wait()
    loads[1].wait()
    length = len_ref[0, 0]
    live = length + SUMM
    r = iota((SLOT, tokens), 0)
    pick = jnp.where((iota((SLOT, tokens), 1) == length + r) & (r < SUMM), 1.0, 0.0).astype(BF16)
    own_k = dot(pick, k_ref[...]).astype(BF16)
    own_v = dot(pick, v_ref[...]).astype(BF16)
    for h in range(kv):
        own[h, 0:SLOT, :] = own_k[:, h * D:(h + 1) * D]
        own[h, SLOT:2 * SLOT, :] = own_v[:, h * D:(h + 1) * D]

    i = iota((nmem, tokens), 0)
    mask_ref[0:nmem, :] = jnp.where(((i >> 6) < me) & ((i & 63) < SUMM), 1.0, 0.0)
    p = iota((tokens, tokens), 0)
    t = iota((tokens, tokens), 1)
    mask_ref[nmem:nmem + tokens, :] = jnp.where((p <= t) & (p < live), 1.0, 0.0)

    pl.semaphore_wait(barrier, ndp - 1 + nctx - 1)

    def forward(h, k):
        return pltpu.make_async_remote_copy(
            src_ref=own.at[h], dst_ref=mem.at[h, me],
            send_sem=fs_sem.at[h, k], recv_sem=fr_sem.at[h, k],
            device_id=(dp, lax.rem(me + k, nctx)), device_id_type=MESH)

    for h in range(kv):
        for k in range(1, nctx):
            @pl.when(me + k < nctx)
            def _():
                forward(h, k).start()

    chunk = hid_ref.shape[1] // ndp
    loads[2].wait()

    def columns(d):
        return pl.ds(pl.multiple_of(d * chunk, 128), chunk)

    def exchange(k):
        to = lax.rem(dp + k, ndp)
        return pltpu.make_async_remote_copy(
            src_ref=hid_ref.at[:, columns(to)], dst_ref=hx.at[k], send_sem=s0.at[k], recv_sem=r0.at[k],
            device_id=(to, me), device_id_type=MESH)

    for k in range(1, ndp):
        exchange(k).start()

    loads[3].wait()
    low = dot(hid_ref[...], wt_ref[...], 1, 1).astype(BF16)
    loads[4].wait()
    loads[5].wait()
    loads[6].wait()
    row = iota((tokens, D), 0)
    cot_mask = jnp.where(row < live, 1.0, 0.0).astype(BF16)

    def backward(h, j):
        return pltpu.make_async_remote_copy(
            src_ref=out.at[h, j], dst_ref=rcv.at[h, j],
            send_sem=bs_sem.at[h, j], recv_sem=br_sem.at[h, j],
            device_id=(dp, lax.max(me - 1, 0)), device_id_type=MESH)

    def chain(h):
        for j in range(nctx - 1):
            @pl.when((me < nctx - 1) & (j <= me))
            def _():
                backward(h, j).wait_recv()

            @pl.when((me < nctx - 1) & (j < me))
            def _():
                out[h, j] = pack_terms(loc[h, j] + unpack_terms(rcv[h, j]))
                backward(h, j).start()

    pr = iota((tokens, 128), 0) - length
    cr = iota((tokens, 128), 1)
    put_k = jnp.where((pr == cr) & (cr < SUMM), 1.0, 0.0).astype(BF16)
    put_v = jnp.where((pr == cr - SLOT) & (pr >= 0) & (pr < SUMM), 1.0, 0.0).astype(BF16)
    key_parts, value_parts = [], []

    def finish(h, back_sum):
        cols = slice(h * D, (h + 1) * D)
        back = unpack_terms(rcv[h, me])
        hi = back.astype(BF16)
        rest = back - hi.astype(F32)
        mid = rest.astype(BF16)
        lo = (rest - mid.astype(F32)).astype(BF16)
        gv = (value_parts[h] + ((dot(put_v, lo) + dot(put_v, mid)) + dot(put_v, hi))).astype(BF16)
        gv_ref[:, cols] = gv
        back_sum = back_sum + dot(up_ref[:, cols], gv, 1, 1)
        gk = key_parts[h] + ((dot(put_k, lo) + dot(put_k, mid)) + dot(put_k, hi))
        gk_ref[:, cols] = gk.astype(BF16)
        up_part = dot(low, gv, 0, 0)
        for a in range(rank // 8):
            n = a * kv + h
            at = (n % ups_each) * 8
            pay[n // ups_each, at:at + 8, :] = up_part[a * 8:a * 8 + 8]
        return back_sum

    rank = up_ref.shape[0]
    back_sum = jnp.zeros((rank, tokens), F32)
    for n in range(rank // 8 * kv, ndp * ups_each):
        at = (n % ups_each) * 8
        pay[n // ups_each, at:at + 8, :] = jnp.zeros((8, 128), F32)

    for h in range(kv):
        for k in range(1, nctx):
            @pl.when(me >= k)
            def _():
                forward(h, k).wait_recv()
        cols = slice(h * D, (h + 1) * D)
        keys = jnp.concatenate([mem[h, j, 0:SLOT, :] for j in range(nctx)] + [k_ref[:, cols]], 0)
        vals = jnp.concatenate([mem[h, j, SLOT:2 * SLOT, :] for j in range(nctx)] + [v_ref[:, cols]], 0)
        heads = [h * groups + g for g in range(groups)]
        q = jnp.concatenate([q_ref[:, a * D:(a + 1) * D] for a in heads], 0)
        c = jnp.concatenate([cot_ref[:, a * D:(a + 1) * D] * cot_mask for a in heads], 0)
        s_ref[...] = dot(keys, q, 1, 1)
        dp_ref[...] = dot(vals, c, 1, 1)
        for g in range(groups):
            lanes = slice(g * tokens, (g + 1) * tokens)
            e = jnp.exp(s_ref[:, lanes] * scale) * mask_ref[...]
            attend = e * (1.0 / jnp.sum(e, 0, keepdims=True))
            grad = dp_ref[:, lanes]
            dot_row = jnp.sum(attend * grad, 0, keepdims=True)
            p_ref[:, lanes] = attend.astype(BF16)
            ds_ref[:, lanes] = (attend * (grad - dot_row)).astype(BF16)
        ds = ds_ref[...]
        dk = dot(ds, q) * scale
        dv = dot(p_ref[...], c)
        for j in range(nctx - 1):
            at = j * SLOT
            loc[h, j, 0:SLOT, :] = dk[at:at + SLOT]
            loc[h, j, SLOT:2 * SLOT, :] = dv[at:at + SLOT]

            @pl.when(me == nctx - 1)
            def _():
                out[h, j] = pack_terms(loc[h, j])
                backward(h, j).start()
        key_parts.append(dk[nmem:])
        value_parts.append(dv[nmem:])
        dq = dot(ds, keys, 0, 0) * scale
        for g, a in enumerate(heads):
            gq_ref[:, a * D:(a + 1) * D] = dq[g * tokens:(g + 1) * tokens].astype(BF16)
        if h > 0:
            chain(h - 1)
            back_sum = finish(h - 1, back_sum)
    stores[0].start()
    chain(kv - 1)
    back_sum = finish(kv - 1, back_sum)

    bx[0] = back_sum.astype(BF16)

    def tell(k):
        return pltpu.make_async_remote_copy(
            src_ref=bx.at[0], dst_ref=bx.at[k], send_sem=sb.at[k], recv_sem=rb.at[k],
            device_id=(lax.rem(dp + k, ndp), me), device_id_type=MESH)

    def scatter(k):
        to = lax.rem(dp + k, ndp)
        return pltpu.make_async_remote_copy(
            src_ref=pay.at[to], dst_ref=rs.at[k], send_sem=s1.at[k], recv_sem=r1.at[k],
            device_id=(to, me), device_id_type=MESH)

    def spread(k):
        return pltpu.make_async_remote_copy(
            src_ref=zbuf.at[me], dst_ref=zbuf.at[me], send_sem=s2.at[k], recv_sem=r2.at[k],
            device_id=(dp, lax.rem(me + k, nctx)), device_id_type=MESH)

    def spread_in(k):
        come = lax.rem(me + nctx - k, nctx)
        return pltpu.make_async_remote_copy(
            src_ref=zbuf.at[come], dst_ref=zbuf.at[come], send_sem=s2.at[k], recv_sem=r2.at[k],
            device_id=(dp, come), device_id_type=MESH)

    def gather(k):
        return pltpu.make_async_remote_copy(
            src_ref=gat.at[dp], dst_ref=gat.at[dp], send_sem=s3.at[k], recv_sem=r3.at[k],
            device_id=(lax.rem(dp + k, ndp), me), device_id_type=MESH)

    def gather_in(k):
        come = lax.rem(dp + ndp - k, ndp)
        return pltpu.make_async_remote_copy(
            src_ref=gat.at[come], dst_ref=gat.at[come], send_sem=s3.at[k], recv_sem=r3.at[k],
            device_id=(come, me), device_id_type=MESH)

    for k in range(1, ndp):
        tell(k).start()
    for k in range(1, ndp):
        scatter(k).start()
    stores[1].start()
    stores[2].start()
    down = dot(bx[0], hid_ref[:, columns(dp)])
    up_sum = pay[dp]
    for k in range(1, ndp):
        exchange(k).wait_recv()
        tell(k).wait_recv()
        down = down + dot(bx[k], hx[k])
    for k in range(1, ndp):
        scatter(k).wait_recv()
        up_sum = up_sum + rs[k]
    blocks = chunk // 128
    first = blocks * rank
    rows = first + ups_each * 8
    sums = jnp.concatenate([down[:, b * 128:(b + 1) * 128] for b in range(blocks)] + [up_sum], 0)
    zbuf[me] = pack_sums(sums, first)
    for k in range(1, nctx):
        spread(k).start()
    for k in range(1, nctx):
        spread_in(k).wait_recv()
    total = unpack_sums(zbuf[0], first, rows)
    for j in range(1, nctx):
        total = total + unpack_sums(zbuf[j], first, rows)
    gat[dp] = pack_sums(total * (ADAPTER_SCALE / (ndp * nctx)), first)
    for k in range(1, ndp):
        gather(k).start()
    for d in range(ndp):
        if d < ndp - 1:
            gather_in(d + 1).wait_recv()
    for d in range(ndp):
        whole = unpack_sums(gat[d], first, rows)
        for b in range(blocks):
            at = d * chunk + b * 128
            down_ref[:, at:at + 128] = whole[b * rank:(b + 1) * rank]
        for u in range(ups_each):
            n = d * ups_each + u
            if n < rank // 8 * kv:
                at = blocks * rank + u * 8
                a, b = n // kv * 8, n % kv * 128
                upg_ref[a:a + 8, b:b + 128] = whole[at:at + 8]

    stores[3].start()
    stores[4].start()

    for h in range(kv):
        for k in range(1, nctx):
            @pl.when(me + k < nctx)
            def _():
                forward(h, k).wait_send()
        for j in range(nctx - 1):
            @pl.when(j < me)
            def _():
                backward(h, j).wait_send()
    for k in range(1, ndp):
        exchange(k).wait_send()
        tell(k).wait_send()
        scatter(k).wait_send()
        gather(k).wait_send()
    for k in range(1, nctx):
        spread(k).wait_send()
    for c in stores:
        c.wait()


def write_out(*refs):
    ins, outs, held, sem_in, sem_out = refs[:5], refs[5:10], refs[10:15], refs[15], refs[16]
    loads = [pltpu.make_async_copy(ins[i], held[i], sem_in.at[i]) for i in range(5)]
    stores = [pltpu.make_async_copy(held[i], outs[i], sem_out.at[i]) for i in range(5)]
    for c in loads:
        c.start()
    for i in range(5):
        loads[i].wait()
        stores[i].start()
    for c in stores:
        c.wait()


def per_device(ndp, nctx, queries, rotated_key_rows, values, cotangent, hidden, down_w, up_w, seg_len):
    q, k, v, cot, hid = (a[0, 0] for a in (queries, rotated_key_rows, values, cotangent, hidden))
    tokens, width = k.shape
    kv = width // HEAD_SIZE
    groups = q.shape[1] // width
    model = hid.shape[1]
    rank = up_w.shape[0]
    D = HEAD_SIZE
    ups_each = -(-(rank // 8 * kv) // ndp)
    chunk = model // ndp
    rows = -(-(chunk // 128 * rank + ups_each * 8 + 8) // 16) * 16
    nkeys = nctx * SLOT + tokens
    lanes = groups * tokens
    hbm = pl.BlockSpec(memory_space=pl.ANY)
    sm = pl.BlockSpec(memory_space=pltpu.SMEM)
    dma = pltpu.SemaphoreType.DMA
    results = pl.pallas_call(
        functools.partial(kernel, ndp, nctx, kv, groups, tokens, ups_each),
        out_shape=(
            jax.ShapeDtypeStruct(q.shape, BF16),
            jax.ShapeDtypeStruct(k.shape, BF16),
            jax.ShapeDtypeStruct(v.shape, BF16),
            jax.ShapeDtypeStruct((rank, model), F32),
            jax.ShapeDtypeStruct((rank, width), F32),
        ),
        in_specs=[sm] + [hbm] * 7,
        out_specs=(hbm,) * 5,
        scratch_shapes=[
            pltpu.VMEM(q.shape, BF16),
            pltpu.VMEM(k.shape, BF16),
            pltpu.VMEM(v.shape, BF16),
            pltpu.VMEM((rank, model), F32),
            pltpu.VMEM((rank, width), F32),
            pltpu.VMEM(k.shape, BF16),
            pltpu.VMEM(v.shape, BF16),
            pltpu.VMEM((rank, model), BF16),
            pltpu.VMEM((rank, width), BF16),
            pltpu.VMEM(q.shape, BF16),
            pltpu.VMEM(cot.shape, BF16),
            pltpu.VMEM(hid.shape, BF16),
            pltpu.VMEM((ndp, tokens, chunk), BF16),
            pltpu.VMEM((ndp, rank, tokens), BF16),
            pltpu.VMEM((kv, 2 * SLOT, D), BF16),
            pltpu.VMEM((kv, nctx, 2 * SLOT, D), BF16),
            pltpu.VMEM((kv, nctx, 2 * SLOT, D), F32),
            pltpu.VMEM((kv, nctx, BACK, D), jnp.int16),
            pltpu.VMEM((kv, nctx, BACK, D), jnp.int16),
            pltpu.VMEM((nkeys, tokens), F32),
            pltpu.VMEM((nkeys, lanes), F32),
            pltpu.VMEM((nkeys, lanes), F32),
            pltpu.VMEM((nkeys, lanes), BF16),
            pltpu.VMEM((nkeys, lanes), BF16),
            pltpu.VMEM((ndp, ups_each * 8, 128), F32),
            pltpu.VMEM((ndp, ups_each * 8, 128), F32),
            pltpu.VMEM((nctx, rows, 128), jnp.int16),
            pltpu.VMEM((ndp, rows, 128), jnp.int16),
            dma((7,)), dma((5,)),
            dma((kv, nctx)), dma((kv, nctx)),
            dma((kv, nctx)), dma((kv, nctx)),
            dma((ndp,)), dma((ndp,)),
            dma((ndp,)), dma((ndp,)),
            dma((ndp,)), dma((ndp,)),
            dma((nctx,)), dma((nctx,)),
            dma((ndp,)), dma((ndp,)),
        ],
        compiler_params=pltpu.CompilerParams(
            collective_id=0, has_side_effects=True, vmem_limit_bytes=62 * 1024 * 1024),
    )(seg_len, k, v, down_w.T, up_w, q, cot, hid)
    gq, gk, gv, down, upg = pl.pallas_call(
        write_out,
        out_shape=tuple(jax.ShapeDtypeStruct(a.shape, a.dtype) for a in results),
        in_specs=[hbm] * 5,
        out_specs=(hbm,) * 5,
        scratch_shapes=[pltpu.VMEM(a.shape, a.dtype) for a in results] + [dma((5,)), dma((5,))],
        compiler_params=pltpu.CompilerParams(vmem_limit_bytes=62 * 1024 * 1024),
    )(*results)
    return gq[None, None], gk[None, None], gv[None, None], down.T, upg


def solution(mesh):
    split = P("dp", "ctx", None, None)
    return jax.shard_map(
        functools.partial(per_device, mesh.shape["dp"], mesh.shape["ctx"]),
        mesh=mesh,
        in_specs=(split,) * 5 + (P(), P(), P("dp", "ctx")),
        out_specs=(split,) * 3 + (P(), P()),
        check_vma=False,
    )
```

```python
import functools
import math

import jax
import jax.numpy as jnp
from jax import lax
from jax.experimental import pallas as pl
from jax.experimental.pallas import tpu as pltpu
from jax.sharding import PartitionSpec as P

HEAD_SIZE = 128
SUMM = 50
SLOT = 64
SENT = 112
BACK = 112
STEPS = 64.0
TOP = 32000.0
ADAPTER_SCALE = 2.0
MESH = pl.DeviceIdType.MESH
F32 = jnp.float32
BF16 = jnp.bfloat16


def iota(shape, dim):
    return lax.broadcasted_iota(jnp.int32, shape, dim)


def dot(a, b, ca=1, cb=0):
    return lax.dot_general(a, b, (((ca,), (cb,)), ((), ())), preferred_element_type=F32)


def code(x):
    most = jnp.max(jnp.abs(x), 0, keepdims=True)
    level = jnp.ceil(jnp.log(jnp.maximum(most, 1e-30)) * (STEPS / math.log(2.0))) + 1.0
    return jnp.round(x * (TOP * jnp.exp(level * (-math.log(2.0) / STEPS)))), level


def scale_of(level):
    return jnp.exp(level * (math.log(2.0) / STEPS)) * (1.0 / TOP)


def level_rows(first, second, rows):
    at = iota((rows, 128), 0)
    return jnp.where(at == 0, first, jnp.where(at == 1, second, 0.0))


def to_wire(x):
    return x.astype(jnp.int32).astype(jnp.int16)


def from_wire(x):
    return x.astype(jnp.int32).astype(F32)


def pack_terms(both):
    k, level_k = code(both[0:SLOT])
    v, level_v = code(both[SLOT:2 * SLOT])
    v = pltpu.roll(v, 2, 0)
    return to_wire(jnp.concatenate(
        [k[0:48], k[48:56] + v[0:8], v[8:56], level_rows(level_k, level_v, 8)], 0))


def unpack_terms(wire):
    x = from_wire(wire)
    keep = iota((SLOT, 128), 0) < SUMM
    k = jnp.where(keep, x[0:SLOT] * scale_of(x[104:105]), 0.0)
    v = jnp.where(keep, pltpu.roll(x[48:112], SLOT - 2, 0) * scale_of(x[105:106]), 0.0)
    return jnp.concatenate([k, v], 0)


def pack_sums(x, first):
    a, level_a = code(x[:first])
    b, level_b = code(x[first:])
    wire = [a, b, level_rows(level_a, level_b, 8)]
    if (x.shape[0] + 8) % 16:
        wire.append(jnp.zeros((8, 128), F32))
    return to_wire(jnp.concatenate(wire, 0))


def unpack_sums(wire, first, rows):
    x = from_wire(wire)
    return jnp.concatenate(
        [x[:first] * scale_of(x[rows:rows + 1]), x[first:rows] * scale_of(x[rows + 1:rows + 2])], 0)


def kernel(
    ndp, nctx, kv, groups, tokens, ups_each,
    len_ref, k_hbm, v_hbm, wt_hbm, up_hbm, q_hbm, cot_hbm, hid_hbm,
    gq_hbm, gk_hbm, gv_hbm, down_hbm, upg_hbm,
    gq_ref, gk_ref, gv_ref, down_ref, upg_ref,
    k_ref, v_ref, wt_ref, up_ref, q_ref, cot_ref, hid_ref, hx, bx, own, mem, loc, out, rcv, mask_ref, s_ref, dp_ref, p_ref, ds_ref,
    pay, rs, zbuf, gat,
    load_sem, store_sem, fs_sem, fr_sem, bs_sem, br_sem, s0, r0, sb, rb, s1, r1, s2, r2, s3, r3,
):
    D = HEAD_SIZE
    nmem = nctx * SLOT
    scale = 1.0 / math.sqrt(D)
    dp = lax.axis_index("dp")
    me = lax.axis_index("ctx")
    loads = [
        pltpu.make_async_copy(src, dst, load_sem.at[i])
        for i, (src, dst) in enumerate((
            (k_hbm, k_ref), (v_hbm, v_ref), (hid_hbm, hid_ref), (wt_hbm, wt_ref),
            (q_hbm, q_ref), (cot_hbm, cot_ref), (up_hbm, up_ref)))
    ]
    for c in loads:
        c.start()
    stores = [
        pltpu.make_async_copy(src, dst, store_sem.at[i])
        for i, (src, dst) in enumerate((
            (gq_ref, gq_hbm), (gk_ref, gk_hbm), (gv_ref, gv_hbm), (down_ref, down_hbm), (upg_ref, upg_hbm)))
    ]

    mem[...] = jnp.zeros_like(mem)
    rcv[...] = jnp.zeros_like(rcv)

    barrier = pltpu.get_barrier_semaphore()
    for k in range(1, ndp):
        pl.semaphore_signal(barrier, inc=1, device_id=(lax.rem(dp + k, ndp), me), device_id_type=MESH)
    for k in range(1, nctx):
        pl.semaphore_signal(barrier, inc=1, device_id=(dp, lax.rem(me + k, nctx)), device_id_type=MESH)

    loads[0].wait()
    loads[1].wait()
    length = len_ref[0, 0]
    live = length + SUMM
    r = iota((SENT, tokens), 0)
    at = iota((SENT, tokens), 1) - length
    pick_k = jnp.where((at == r) & (r < SUMM), 1.0, 0.0).astype(BF16)
    pick_v = jnp.where((at == r - SUMM) & (at >= 0) & (at < SUMM), 1.0, 0.0).astype(BF16)
    sent = (dot(pick_k, k_ref[...]) + dot(pick_v, v_ref[...])).astype(BF16)
    for h in range(kv):
        own[h, :, :] = sent[:, h * D:(h + 1) * D]

    i = iota((nmem, tokens), 0)
    mask_ref[0:nmem, :] = jnp.where(((i >> 6) < me) & ((i & 63) < SUMM), 1.0, 0.0)
    p = iota((tokens, tokens), 0)
    t = iota((tokens, tokens), 1)
    mask_ref[nmem:nmem + tokens, :] = jnp.where((p <= t) & (p < live), 1.0, 0.0)

    pl.semaphore_wait(barrier, ndp - 1 + nctx - 1)

    def forward(h, k):
        return pltpu.make_async_remote_copy(
            src_ref=own.at[h], dst_ref=mem.at[h, me],
            send_sem=fs_sem.at[h, k], recv_sem=fr_sem.at[h, k],
            device_id=(dp, lax.rem(me + k, nctx)), device_id_type=MESH)

    for h in range(kv):
        for k in range(1, nctx):
            @pl.when(me + k < nctx)
            def _():
                forward(h, k).start()

    chunk = hid_ref.shape[1] // ndp
    loads[2].wait()

    def columns(d):
        return pl.ds(pl.multiple_of(d * chunk, 128), chunk)

    def exchange(k):
        to = lax.rem(dp + k, ndp)
        return pltpu.make_async_remote_copy(
            src_ref=hid_ref.at[:, columns(to)], dst_ref=hx.at[k], send_sem=s0.at[k], recv_sem=r0.at[k],
            device_id=(to, me), device_id_type=MESH)

    for k in range(1, ndp):
        exchange(k).start()

    loads[4].wait()
    loads[5].wait()
    row = iota((tokens, D), 0)
    cot_mask = jnp.where(row < live, 1.0, 0.0).astype(BF16)

    def backward(h, j):
        return pltpu.make_async_remote_copy(
            src_ref=out.at[h, j], dst_ref=rcv.at[h, j],
            send_sem=bs_sem.at[h, j], recv_sem=br_sem.at[h, j],
            device_id=(dp, lax.max(me - 1, 0)), device_id_type=MESH)

    def chain(h):
        for j in range(nctx - 1):
            @pl.when((me < nctx - 1) & (j <= me))
            def _():
                backward(h, j).wait_recv()

            @pl.when((me < nctx - 1) & (j < me))
            def _():
                out[h, j] = pack_terms(loc[h, j] + unpack_terms(rcv[h, j]))
                backward(h, j).start()

    pr = iota((tokens, 128), 0) - length
    cr = iota((tokens, 128), 1)
    put_k = jnp.where((pr == cr) & (cr < SUMM), 1.0, 0.0).astype(BF16)
    put_v = jnp.where((pr == cr - SLOT) & (pr >= 0) & (pr < SUMM), 1.0, 0.0).astype(BF16)
    key_parts, value_parts = [], []

    def head_rows(h):
        heads = [h * groups + g for g in range(groups)]
        q = jnp.concatenate([q_ref[:, a * D:(a + 1) * D] for a in heads], 0)
        c = jnp.concatenate([cot_ref[:, a * D:(a + 1) * D] * cot_mask for a in heads], 0)
        return q, c

    def own_scores(h):
        cols = slice(h * D, (h + 1) * D)
        q, c = head_rows(h)
        s = dot(k_ref[:, cols], q, 1, 1)
        dp_ref[h, nmem:, :] = dot(v_ref[:, cols], c, 1, 1)
        for g in range(groups):
            lanes = slice(g * tokens, (g + 1) * tokens)
            s_ref[h, nmem:, lanes] = jnp.exp(s[:, lanes] * scale) * mask_ref[nmem:, :]

    def query_grads(h):
        cols = slice(h * D, (h + 1) * D)
        keys = jnp.concatenate([mem[h, j, 0:SLOT, :] for j in range(nctx)] + [k_ref[:, cols]], 0)
        dq = dot(ds_ref[h], keys, 0, 0) * scale
        for g in range(groups):
            a = h * groups + g
            gq_ref[:, a * D:(a + 1) * D] = dq[g * tokens:(g + 1) * tokens].astype(BF16)

    def finish(h, back_sum, low):
        cols = slice(h * D, (h + 1) * D)
        back = unpack_terms(rcv[h, me])
        hi = back.astype(BF16)
        rest = back - hi.astype(F32)
        mid = rest.astype(BF16)
        lo = (rest - mid.astype(F32)).astype(BF16)
        gv = (value_parts[h] + ((dot(put_v, lo) + dot(put_v, mid)) + dot(put_v, hi))).astype(BF16)
        gv_ref[:, cols] = gv
        back_sum = back_sum + dot(up_ref[:, cols], gv, 1, 1)
        gk = key_parts[h] + ((dot(put_k, lo) + dot(put_k, mid)) + dot(put_k, hi))
        gk_ref[:, cols] = gk.astype(BF16)
        up_part = dot(low, gv, 0, 0)
        for a in range(rank // 8):
            n = a * kv + h
            at = (n % ups_each) * 8
            pay[n // ups_each, at:at + 8, :] = up_part[a * 8:a * 8 + 8]
        return back_sum

    rank = up_ref.shape[0]
    back_sum = jnp.zeros((rank, tokens), F32)
    for n in range(rank // 8 * kv, ndp * ups_each):
        at = (n % ups_each) * 8
        pay[n // ups_each, at:at + 8, :] = jnp.zeros((8, 128), F32)

    own_scores(0)
    own_scores(1)
    for h in range(kv):
        for k in range(1, nctx):
            @pl.when(me >= k)
            def _():
                forward(h, k).wait_recv()
        q, c = head_rows(h)
        keys = jnp.concatenate([mem[h, j, 0:SLOT, :] for j in range(nctx)], 0)
        vals = jnp.concatenate(
            [pltpu.roll(mem[h, j, SENT - SLOT:SENT, :].astype(F32), SLOT - 2, 0).astype(BF16)
             for j in range(nctx)], 0)
        s_ref[h, 0:nmem, :] = dot(keys, q, 1, 1)
        dp_ref[h, 0:nmem, :] = dot(vals, c, 1, 1)
        for g in range(groups):
            lanes = slice(g * tokens, (g + 1) * tokens)
            e = jnp.exp(s_ref[h, 0:nmem, lanes] * scale) * mask_ref[0:nmem, :]
            e = jnp.concatenate([e, s_ref[h, nmem:, lanes]], 0)
            attend = e * (1.0 / jnp.sum(e, 0, keepdims=True))
            grad = dp_ref[h, :, lanes]
            dot_row = jnp.sum(attend * grad, 0, keepdims=True)
            p_ref[:, lanes] = attend.astype(BF16)
            ds_ref[h, :, lanes] = (attend * (grad - dot_row)).astype(BF16)
        dk = dot(ds_ref[h, 0:nmem, :], q) * scale
        dv = dot(p_ref[0:nmem, :], c)
        for j in range(nctx - 1):
            at = j * SLOT
            loc[h, j, 0:SLOT, :] = dk[at:at + SLOT]
            loc[h, j, SLOT:2 * SLOT, :] = dv[at:at + SLOT]

            @pl.when(me == nctx - 1)
            def _():
                out[h, j] = pack_terms(loc[h, j])
                backward(h, j).start()
        if h > 0:
            chain(h - 1)
        key_parts.append(dot(ds_ref[h, nmem:, :], q) * scale)
        value_parts.append(dot(p_ref[nmem:, :], c))
        if h + 2 < kv:
            own_scores(h + 2)
        if h == 0:
            loads[3].wait()
            loads[6].wait()
            low = dot(hid_ref[...], wt_ref[...], 1, 1).astype(BF16)
        else:
            back_sum = finish(h - 1, back_sum, low)
    chain(kv - 1)
    back_sum = finish(kv - 1, back_sum, low)

    bx[0] = back_sum.astype(BF16)

    def tell(k):
        return pltpu.make_async_remote_copy(
            src_ref=bx.at[0], dst_ref=bx.at[k], send_sem=sb.at[k], recv_sem=rb.at[k],
            device_id=(lax.rem(dp + k, ndp), me), device_id_type=MESH)

    def scatter(k):
        to = lax.rem(dp + k, ndp)
        return pltpu.make_async_remote_copy(
            src_ref=pay.at[to], dst_ref=rs.at[k], send_sem=s1.at[k], recv_sem=r1.at[k],
            device_id=(to, me), device_id_type=MESH)

    def spread(k):
        return pltpu.make_async_remote_copy(
            src_ref=zbuf.at[me], dst_ref=zbuf.at[me], send_sem=s2.at[k], recv_sem=r2.at[k],
            device_id=(dp, lax.rem(me + k, nctx)), device_id_type=MESH)

    def spread_in(k):
        come = lax.rem(me + nctx - k, nctx)
        return pltpu.make_async_remote_copy(
            src_ref=zbuf.at[come], dst_ref=zbuf.at[come], send_sem=s2.at[k], recv_sem=r2.at[k],
            device_id=(dp, come), device_id_type=MESH)

    def gather(k):
        return pltpu.make_async_remote_copy(
            src_ref=gat.at[dp], dst_ref=gat.at[dp], send_sem=s3.at[k], recv_sem=r3.at[k],
            device_id=(lax.rem(dp + k, ndp), me), device_id_type=MESH)

    def gather_in(k):
        come = lax.rem(dp + ndp - k, ndp)
        return pltpu.make_async_remote_copy(
            src_ref=gat.at[come], dst_ref=gat.at[come], send_sem=s3.at[k], recv_sem=r3.at[k],
            device_id=(come, me), device_id_type=MESH)

    for k in range(1, ndp):
        tell(k).start()
    for k in range(1, ndp):
        scatter(k).start()
    stores[1].start()
    stores[2].start()
    query_grads(0)
    query_grads(1)
    down = dot(bx[0], hid_ref[:, columns(dp)])
    up_sum = pay[dp]
    for k in range(1, ndp):
        exchange(k).wait_recv()
        tell(k).wait_recv()
        down = down + dot(bx[k], hx[k])
    for k in range(1, ndp):
        scatter(k).wait_recv()
        up_sum = up_sum + rs[k]
    blocks = chunk // 128
    first = blocks * rank
    rows = first + ups_each * 8
    sums = jnp.concatenate([down[:, b * 128:(b + 1) * 128] for b in range(blocks)] + [up_sum], 0)
    zbuf[me] = pack_sums(sums, first)
    for k in range(1, nctx):
        spread(k).start()
    for h in range(2, kv):
        query_grads(h)
    stores[0].start()
    for k in range(1, nctx):
        spread_in(k).wait_recv()
    total = unpack_sums(zbuf[0], first, rows)
    for j in range(1, nctx):
        total = total + unpack_sums(zbuf[j], first, rows)
    gat[dp] = pack_sums(total * (ADAPTER_SCALE / (ndp * nctx)), first)
    for k in range(1, ndp):
        gather(k).start()
    for d in range(ndp):
        if d < ndp - 1:
            gather_in(d + 1).wait_recv()
    for d in range(ndp):
        whole = unpack_sums(gat[d], first, rows)
        for b in range(blocks):
            at = d * chunk + b * 128
            down_ref[:, at:at + 128] = whole[b * rank:(b + 1) * rank]
        for u in range(ups_each):
            n = d * ups_each + u
            if n < rank // 8 * kv:
                at = blocks * rank + u * 8
                a, b = n // kv * 8, n % kv * 128
                upg_ref[a:a + 8, b:b + 128] = whole[at:at + 8]

    stores[3].start()
    stores[4].start()

    for h in range(kv):
        for k in range(1, nctx):
            @pl.when(me + k < nctx)
            def _():
                forward(h, k).wait_send()
        for j in range(nctx - 1):
            @pl.when(j < me)
            def _():
                backward(h, j).wait_send()
    for k in range(1, ndp):
        exchange(k).wait_send()
        tell(k).wait_send()
        scatter(k).wait_send()
        gather(k).wait_send()
    for k in range(1, nctx):
        spread(k).wait_send()
    for c in stores:
        c.wait()


def write_out(*refs):
    ins, outs, held, sem_in, sem_out = refs[:5], refs[5:10], refs[10:15], refs[15], refs[16]
    loads = [pltpu.make_async_copy(ins[i], held[i], sem_in.at[i]) for i in range(5)]
    stores = [pltpu.make_async_copy(held[i], outs[i], sem_out.at[i]) for i in range(5)]
    for c in loads:
        c.start()
    for i in range(5):
        loads[i].wait()
        stores[i].start()
    for c in stores:
        c.wait()


def per_device(ndp, nctx, queries, rotated_key_rows, values, cotangent, hidden, down_w, up_w, seg_len):
    q, k, v, cot, hid = (a[0, 0] for a in (queries, rotated_key_rows, values, cotangent, hidden))
    tokens, width = k.shape
    kv = width // HEAD_SIZE
    groups = q.shape[1] // width
    model = hid.shape[1]
    rank = up_w.shape[0]
    D = HEAD_SIZE
    ups_each = -(-(rank // 8 * kv) // ndp)
    chunk = model // ndp
    rows = -(-(chunk // 128 * rank + ups_each * 8 + 8) // 16) * 16
    nkeys = nctx * SLOT + tokens
    lanes = groups * tokens
    hbm = pl.BlockSpec(memory_space=pl.ANY)
    sm = pl.BlockSpec(memory_space=pltpu.SMEM)
    dma = pltpu.SemaphoreType.DMA
    results = pl.pallas_call(
        functools.partial(kernel, ndp, nctx, kv, groups, tokens, ups_each),
        out_shape=(
            jax.ShapeDtypeStruct(q.shape, BF16),
            jax.ShapeDtypeStruct(k.shape, BF16),
            jax.ShapeDtypeStruct(v.shape, BF16),
            jax.ShapeDtypeStruct((rank, model), F32),
            jax.ShapeDtypeStruct((rank, width), F32),
        ),
        in_specs=[sm] + [hbm] * 7,
        out_specs=(hbm,) * 5,
        scratch_shapes=[
            pltpu.VMEM(q.shape, BF16),
            pltpu.VMEM(k.shape, BF16),
            pltpu.VMEM(v.shape, BF16),
            pltpu.VMEM((rank, model), F32),
            pltpu.VMEM((rank, width), F32),
            pltpu.VMEM(k.shape, BF16),
            pltpu.VMEM(v.shape, BF16),
            pltpu.VMEM((rank, model), BF16),
            pltpu.VMEM((rank, width), BF16),
            pltpu.VMEM(q.shape, BF16),
            pltpu.VMEM(cot.shape, BF16),
            pltpu.VMEM(hid.shape, BF16),
            pltpu.VMEM((ndp, tokens, chunk), BF16),
            pltpu.VMEM((ndp, rank, tokens), BF16),
            pltpu.VMEM((kv, SENT, D), BF16),
            pltpu.VMEM((kv, nctx, SENT, D), BF16),
            pltpu.VMEM((kv, nctx, 2 * SLOT, D), F32),
            pltpu.VMEM((kv, nctx, BACK, D), jnp.int16),
            pltpu.VMEM((kv, nctx, BACK, D), jnp.int16),
            pltpu.VMEM((nkeys, tokens), F32),
            pltpu.VMEM((kv, nkeys, lanes), F32),
            pltpu.VMEM((kv, nkeys, lanes), F32),
            pltpu.VMEM((nkeys, lanes), BF16),
            pltpu.VMEM((kv, nkeys, lanes), BF16),
            pltpu.VMEM((ndp, ups_each * 8, 128), F32),
            pltpu.VMEM((ndp, ups_each * 8, 128), F32),
            pltpu.VMEM((nctx, rows, 128), jnp.int16),
            pltpu.VMEM((ndp, rows, 128), jnp.int16),
            dma((7,)), dma((5,)),
            dma((kv, nctx)), dma((kv, nctx)),
            dma((kv, nctx)), dma((kv, nctx)),
            dma((ndp,)), dma((ndp,)),
            dma((ndp,)), dma((ndp,)),
            dma((ndp,)), dma((ndp,)),
            dma((nctx,)), dma((nctx,)),
            dma((ndp,)), dma((ndp,)),
        ],
        compiler_params=pltpu.CompilerParams(
            collective_id=0, has_side_effects=True, vmem_limit_bytes=62 * 1024 * 1024),
    )(seg_len, k, v, down_w.T, up_w, q, cot, hid)
    gq, gk, gv, down, upg = pl.pallas_call(
        write_out,
        out_shape=tuple(jax.ShapeDtypeStruct(a.shape, a.dtype) for a in results),
        in_specs=[hbm] * 5,
        out_specs=(hbm,) * 5,
        scratch_shapes=[pltpu.VMEM(a.shape, a.dtype) for a in results] + [dma((5,)), dma((5,))],
        compiler_params=pltpu.CompilerParams(vmem_limit_bytes=62 * 1024 * 1024),
    )(*results)
    return gq[None, None], gk[None, None], gv[None, None], down.T, upg


def solution(mesh):
    split = P("dp", "ctx", None, None)
    return jax.shard_map(
        functools.partial(per_device, mesh.shape["dp"], mesh.shape["ctx"]),
        mesh=mesh,
        in_specs=(split,) * 5 + (P(), P(), P("dp", "ctx")),
        out_specs=(split,) * 3 + (P(), P()),
        check_vma=False,
    )
```
